256 devices in a mesh: section: 2 (over y_hi), row: 16 (over z, y_lo), col: 8 (over x, core).
Axes of the slice: x: 4, y: 4 (y_hi: 2, y_lo: 2; y = y_hi * 2 + y_lo), z: 8, core: 2. Of those that a mesh axis runs over, the one named last changes fastest.
Arguments:
- handed: bfloat16 [2, 768, 768, 128], P('section', ('row', 'col')), may hold values from -6 to 6
- residue_mask: int32 [2, 768], P('section'), may hold values 0 or 1
- input_weights: bfloat16 [2, 128, 640], P('section'), may hold values from -0.5 to 0.5
- input_gain: float32 [2, 128], P('section'), may hold values from 0.1 to 1.9
- product_gain: float32 [2, 128], P('section'), may hold values from 0.1 to 1.9
- output_weights: bfloat16 [2, 128, 128], P('section'), may hold values from -0.5 to 0.5
Outputs:
- updated: bfloat16 [2, 768, 768, 128], P('section', 'row', 'col')
The draws below stay inside these ranges and needn't reach their ends.
All inputs are finite; a program needn't handle non-finite values. No bound on the sum of `residue_mask` on one device may be relied on, other than what follows from the above.
Results may differ from the reference program's by a relative error of at most 0.0052.
Values may be sent and summed in bfloat16 or wider, within the bound.
A program may use at most 64 MiB of HBM per device.

```python
import jax
import jax.numpy as jnp
from jax import lax

C = 128
HID = 128
N = 768
N_ROW = 16


def set_ends(values, rng, smallest, top_value):
    shape = values.shape
    spot = [jax.random.randint(jax.random.fold_in(rng, axis), (), 0, shape[axis]) for axis in range(len(shape))]
    values = values.at[tuple(spot)].set(smallest)
    longest = shape.index(max(shape))
    spot[longest] = (spot[longest] + 1) % shape[longest]
    return values.at[tuple(spot)].set(top_value)


def levels(rng, dims, pieces, least, largest):
    factor_of, own = 1.0, jax.random.fold_in(rng, 6)
    for position, shards_of in pieces:
        draws = jnp.exp(jax.random.uniform(jax.random.fold_in(own, position), (shards_of,), jnp.float32, least / len(pieces), largest / len(pieces)))
        factor_of = factor_of * jnp.repeat(draws, dims[position] // shards_of).reshape([-1 if axis == position else 1 for axis in range(len(dims))])
    return factor_of


def gaussian(stream_key, dims, deviation, most, cuts=(), kind=jnp.bfloat16):
    drawn = deviation * jax.random.normal(stream_key, dims, jnp.float32)
    if cuts:
        drawn = drawn * levels(stream_key, dims, cuts, -0.22, 0.18)
    return jnp.clip(drawn, -most, most).astype(kind)


def setup_inputs(seed: int = 0) -> dict:
    keys = jax.random.split(jax.random.key(seed), 7)
    return {
        "handed": gaussian(keys[0], (2, N, N, C), 1.0, 6.0, ((0, 2), (1, 128))),
        "residue_mask": set_ends((jax.random.randint(keys[1], (2, N), 0, 8) < 7).astype(jnp.int32), jax.random.fold_in(keys[1], 1), 0, 1),
        "input_weights": gaussian(keys[2], (2, C, 4 * HID + C), C ** -0.5, 0.5, ((0, 2),)),
        "input_gain": jnp.clip(1.0 + 0.18 * jax.random.normal(keys[3], (2, C), jnp.float32), 0.1, 1.9),
        "product_gain": jnp.clip(1.0 + 0.18 * jax.random.normal(keys[4], (2, HID), jnp.float32), 0.1, 1.9),
        "output_weights": gaussian(keys[5], (2, HID, C), HID ** -0.5, 0.5, ((0, 2),)),
    }


EPS = 1e-05

def norm_last(values, gain):
    center = lax.optimization_barrier(jnp.mean(values, axis=-1, keepdims=True))
    deviate = values - center
    spread = lax.optimization_barrier(jnp.mean(deviate * deviate, axis=-1, keepdims=True))
    return deviate * lax.rsqrt(spread + EPS) * gain

def one_section(arrived, present, weights, first_gain, second_gain, last_weights):
    block = N // N_ROW
    flags = present.astype(jnp.float32)

    def factor_block(block_index):
        begin = (block_index * block).astype(jnp.int32)
        block_rows = lax.dynamic_slice_in_dim(arrived, begin, block, 0).astype(jnp.float32)
        normed = norm_last(block_rows, first_gain).astype(jnp.bfloat16)
        projected = jnp.dot(normed.reshape(-1, C), weights, preferred_element_type=jnp.float32).reshape(block, N, -1)
        row_flags = lax.dynamic_slice_in_dim(flags, begin, block, 0)
        pair_mask = (row_flags[:, None] * flags[None, :])[:, :, None]
        left_factor = jax.nn.sigmoid(projected[..., 0:HID]) * projected[..., HID:2 * HID] * pair_mask
        right_factor = jax.nn.sigmoid(projected[..., 2 * HID:3 * HID]) * projected[..., 3 * HID:4 * HID] * pair_mask
        return (left_factor.astype(jnp.bfloat16), right_factor.astype(jnp.bfloat16))
    left_all, right_all = lax.map(factor_block, jnp.arange(N_ROW, dtype=jnp.int32))
    left_all = left_all.reshape(N, N, HID).transpose(2, 0, 1)
    right_all = right_all.reshape(N, N, HID).transpose(2, 0, 1)

    def channel_product(operands):
        return jnp.dot(operands[0].astype(jnp.float32), operands[1].astype(jnp.float32).T, preferred_element_type=jnp.float32).astype(jnp.bfloat16)
    products = lax.map(channel_product, (left_all, right_all)).transpose(1, 2, 0)

    def finish_block(block_index):
        begin = (block_index * block).astype(jnp.int32)
        block_rows = lax.dynamic_slice_in_dim(arrived, begin, block, 0).astype(jnp.float32)
        normed = norm_last(block_rows, first_gain).astype(jnp.bfloat16).reshape(-1, C)
        gating = jnp.dot(normed, weights[:, 4 * HID:], preferred_element_type=jnp.float32)
        block_prod = lax.dynamic_slice_in_dim(products, begin, block, 0).astype(jnp.float32)
        prod_norm = norm_last(block_prod, second_gain).astype(jnp.bfloat16).reshape(-1, HID)
        update = jnp.dot(prod_norm, last_weights, preferred_element_type=jnp.float32)
        result = block_rows.reshape(-1, C) + jax.nn.sigmoid(gating) * update
        return result.astype(jnp.bfloat16).reshape(block, N, C)
    return lax.map(finish_block, jnp.arange(N_ROW, dtype=jnp.int32)).reshape(N, N, C)

def reference(handed, residue_mask, input_weights, input_gain, product_gain, output_weights):
    results = []
    for section_index in range(2):
        other = 1 - section_index
        results.append(one_section(handed[other], residue_mask[other], input_weights[section_index], input_gain[section_index], product_gain[section_index], output_weights[section_index]))
    return jnp.stack(results)
```

```python
import functools

import jax
import jax.numpy as jnp
from jax import lax
from jax.experimental import pallas as pl
from jax.experimental.pallas import tpu as pltpu
from jax.sharding import PartitionSpec as P

EPS = 1e-05
MESH = pl.DeviceIdType.MESH


def from_behind(shard, axis, by):
    size = lax.axis_size(axis)
    return lax.ppermute(shard, axis, [(i, (i + by) % size) for i in range(size)])


def norm_rows(values, gain):
    center = jnp.mean(values, axis=-1, keepdims=True)
    deviate = values - center
    spread = jnp.mean(deviate * deviate, axis=-1, keepdims=True)
    return deviate * lax.rsqrt(spread + EPS) * gain


def exchange_kernel(n_row, n_col, x_ref, o_ref, send_sem, recv_sem):
    section = lax.axis_index("section")
    me = lax.axis_index("row") * n_col + lax.axis_index("col")
    total = n_row * n_col

    def device(d):
        t = lax.rem(me + d, total)
        return t, (section, t // n_col, lax.rem(t, n_col))

    barrier = pltpu.get_barrier_semaphore()

    def greet(d, carry):
        pl.semaphore_signal(barrier, inc=1, device_id=device(d)[1], device_id_type=MESH)
        return carry

    lax.fori_loop(1, total, greet, 0)
    own = pltpu.make_async_copy(x_ref.at[me], o_ref.at[me], recv_sem)
    own.start()
    pl.semaphore_wait(barrier, total - 1)

    def send(d, carry):
        t, where = device(d)
        pltpu.make_async_remote_copy(
            src_ref=x_ref.at[t],
            dst_ref=o_ref.at[me],
            send_sem=send_sem,
            recv_sem=recv_sem,
            device_id=where,
            device_id_type=MESH,
        ).start()
        return carry

    lax.fori_loop(1, total, send, 0)
    pltpu.make_async_copy(o_ref, o_ref, recv_sem).wait()
    sent = x_ref.at[pl.ds(0, total - 1)]
    pltpu.make_async_copy(sent, sent, send_sem).wait()


def exchange(blocks, n_row, n_col, cid):
    return pl.pallas_call(
        functools.partial(exchange_kernel, n_row, n_col),
        out_shape=jax.ShapeDtypeStruct(blocks.shape, blocks.dtype),
        in_specs=[pl.BlockSpec(memory_space=pltpu.VMEM)],
        out_specs=pl.BlockSpec(memory_space=pltpu.VMEM),
        scratch_shapes=[pltpu.SemaphoreType.DMA, pltpu.SemaphoreType.DMA],
        compiler_params=pltpu.CompilerParams(
            collective_id=cid, has_side_effects=True, vmem_limit_bytes=40 * 2**20
        ),
    )(blocks)


def local(n_row, n_col, handed, residue_mask, input_weights, input_gain, product_gain, output_weights):
    arrived, present = from_behind((handed, residue_mask.astype(jnp.bfloat16)), "section", 1)
    arrived = arrived[0]
    present = present[0].astype(jnp.float32)
    weights = input_weights[0]
    last_weights = output_weights[0]
    first_gain = input_gain[0]
    second_gain = product_gain[0]
    hidden = last_weights.shape[0]
    rows, size, channels = arrived.shape
    me = lax.axis_index("row") * n_col + lax.axis_index("col")
    normed = norm_rows(arrived.astype(jnp.float32), first_gain).astype(jnp.bfloat16)
    projected = lax.dot_general(
        weights[:, : 4 * hidden], normed.reshape(-1, channels), (((0,), (1,)), ((), ())),
        preferred_element_type=jnp.float32,
    ).reshape(4, hidden, rows, size)
    flags = lax.dynamic_slice_in_dim(present, me * rows, rows, 0)
    pair_mask = flags[:, None] * present[None, :]
    left = (jax.nn.sigmoid(projected[0]) * projected[1] * pair_mask).astype(jnp.bfloat16)
    right = (jax.nn.sigmoid(projected[2]) * projected[3] * pair_mask).astype(jnp.bfloat16)
    stacked = jnp.stack([left, right], axis=1).reshape(hidden, -1, 128)
    owned = exchange(stacked, n_row, n_col, 1).reshape(hidden, 2, rows, size)
    lefts = owned[:, 0].reshape(size, size)
    rights = owned[:, 1].reshape(size, size)
    product = lax.dot_general(
        lefts, rights, (((1,), (1,)), ((), ())), preferred_element_type=jnp.float32
    ).astype(jnp.bfloat16)
    row_count = size // n_row
    col_count = size // n_col
    blocks = product.reshape(n_row, row_count, n_col, col_count).transpose(0, 2, 1, 3)
    grid = exchange(blocks.reshape(hidden, -1, 128), n_row, n_col, 2).reshape(hidden, row_count, col_count)

    blocked = lax.all_to_all(arrived, "col", split_axis=1, concat_axis=0, tiled=True)
    block_norm = (
        norm_rows(blocked.astype(jnp.float32), first_gain).astype(jnp.bfloat16).reshape(-1, channels)
    )
    gating = jnp.dot(block_norm, weights[:, 4 * hidden :], preferred_element_type=jnp.float32)
    widened = grid.astype(jnp.float32)
    center = jnp.mean(widened, axis=0, keepdims=True)
    deviate = widened - center
    spread = jnp.mean(deviate * deviate, axis=0, keepdims=True)
    prod_norm = (deviate * lax.rsqrt(spread + EPS) * second_gain[:, None, None]).astype(jnp.bfloat16)
    update = lax.dot_general(
        prod_norm.reshape(hidden, -1), last_weights, (((0,), (0,)), ((), ())),
        preferred_element_type=jnp.float32,
    )
    result = blocked.astype(jnp.float32).reshape(-1, channels) + jax.nn.sigmoid(gating) * update
    return result.astype(jnp.bfloat16).reshape(1, row_count, col_count, channels)


def solution(mesh):
    placed = (
        P("section", ("row", "col"), None, None),
        P("section", None),
        P("section", None, None),
        P("section", None),
        P("section", None),
        P("section", None, None),
    )
    return jax.shard_map(
        functools.partial(local, mesh.shape["row"], mesh.shape["col"]),
        mesh=mesh,
        in_specs=placed,
        out_specs=P("section", "row", "col", None),
        check_vma=False,
    )
```

```python
import functools

import jax
import jax.numpy as jnp
from jax import lax
from jax.experimental import pallas as pl
from jax.experimental.pallas import tpu as pltpu
from jax.sharding import PartitionSpec as P

EPS = 1e-05
LANES = 128
MESH = pl.DeviceIdType.MESH
BF16 = jnp.bfloat16
F32 = jnp.float32


def norm(values, gain, axis):
    center = jnp.mean(values, axis=axis, keepdims=True)
    deviate = values - center
    spread = jnp.mean(deviate * deviate, axis=axis, keepdims=True)
    return (deviate * lax.rsqrt(spread + EPS) * gain).astype(BF16)


def wait_for(ref, sem):
    pltpu.make_async_copy(ref, ref, sem).wait()


def kernel(
    n_row, n_col,
    handed, mask, w_in, g_in, g_prod, w_out, out,
    slab, flags, w_cols, g_cols, factor_f32, factor_out, factors, products,
    packed_f32, product_out, product_in, product_f32, block, gate,
    flag_sems, slab_send, slab_recv, factor_send, factor_recv,
    product_send, product_recv, block_send, block_recv,
):
    rows, size, channels = slab.shape
    hidden = w_out.shape[1]
    k_tiles = size // LANES
    devices = n_row * n_col
    row_count, col_count = size // n_row, size // n_col
    parts, _, part_rows = product_out.shape[0], 0, 2 * product_out.shape[2]
    section, row, col = (lax.axis_index(a) for a in ("section", "row", "col"))
    me = row * n_col + col
    partner = (1 - section, row, col)

    def at(t):
        return (section, t // n_col, lax.rem(t, n_col))

    barrier = pltpu.get_barrier_semaphore()
    pl.semaphore_signal(barrier, inc=1, device_id=partner, device_id_type=MESH)

    def greet(d, carry):
        pl.semaphore_signal(barrier, inc=1, device_id=at(lax.rem(me + d, devices)), device_id_type=MESH)
        return carry

    lax.fori_loop(1, devices, greet, 0)
    w_cols[...] = w_in[0].astype(F32).T.astype(BF16)
    g_cols[...] = jnp.broadcast_to(g_prod[...], (LANES, hidden)).T
    pl.semaphore_wait(barrier, devices)

    flag_copy = pltpu.make_async_remote_copy(
        src_ref=mask, dst_ref=flags, send_sem=flag_sems.at[0], recv_sem=flag_sems.at[1],
        device_id=partner, device_id_type=MESH,
    )
    flag_copy.start()

    def tile(kt):
        return pl.ds(pl.multiple_of(kt * LANES, LANES), LANES)

    def slab_copy(kt):
        return pltpu.make_async_remote_copy(
            src_ref=handed.at[0, :, tile(kt)], dst_ref=slab.at[:, tile(kt)],
            send_sem=slab_send, recv_sem=slab_recv.at[kt],
            device_id=partner, device_id_type=MESH,
        )

    slab_copy(0).start()
    slab_copy(1).start()
    flag_copy.wait()

    per_owner = 2 * rows
    factor_rows = factor_out.reshape(k_tiles * devices * per_owner, LANES)
    all_flags = flags[...].astype(F32)
    places = lax.broadcasted_iota(jnp.int32, all_flags.shape, 1)
    own_flags = [
        jnp.sum(jnp.where(places == me * rows + i, all_flags, 0.0), axis=1, keepdims=True)
        for i in range(rows)
    ]

    def factor_step(kt, carry):
        wait_for(slab.at[:, tile(kt)], slab_recv.at[kt])

        @pl.when(kt + 2 < k_tiles)
        def _():
            slab_copy(kt + 2).start()

        k_flags = flags[:, tile(kt)].astype(F32)
        for i in range(rows):
            normed = norm(slab[i, tile(kt), :].astype(F32), g_in[...], 1)
            projected = lax.dot_general(
                w_cols[: 4 * hidden], normed, (((1,), (1,)), ((), ())), preferred_element_type=F32
            )
            pair_flags = k_flags * own_flags[i]
            for side in range(2):
                gates = projected[2 * side * hidden : (2 * side + 1) * hidden]
                values = projected[(2 * side + 1) * hidden : (2 * side + 2) * hidden]
                factor_f32[pl.ds(side * rows + i, hidden, stride=per_owner), :] = (
                    jax.nn.sigmoid(gates) * values * pair_flags
                )
        begin = pl.multiple_of(kt * (devices * per_owner), devices * per_owner)
        factor_rows[pl.ds(begin, devices * per_owner), :] = factor_f32[...].astype(BF16)
        target = factors.at[:, kt, pl.ds(me * (rows // 2), rows // 2)]
        pltpu.make_async_copy(factor_out.at[kt, me], target, factor_recv.at[kt]).start()

        def send(d, c):
            t = lax.rem(me + d, devices)
            pltpu.make_async_remote_copy(
                src_ref=factor_out.at[kt, t], dst_ref=target,
                send_sem=factor_send, recv_sem=factor_recv.at[kt],
                device_id=at(t), device_id_type=MESH,
            ).start()
            return c

        lax.fori_loop(1, devices, send, 0)
        return carry

    lax.fori_loop(0, k_tiles, factor_step, 0)

    def columns(c):
        return pl.ds(pl.multiple_of(c * col_count, col_count), col_count)

    block_rows = block.at[pl.ds(col * rows, rows)]
    pltpu.make_async_copy(slab.at[:, columns(col)], block_rows, block_recv).start()

    def send_block(d, carry):
        c = lax.rem(col + d, n_col)
        pltpu.make_async_remote_copy(
            src_ref=slab.at[:, columns(c)], dst_ref=block_rows,
            send_sem=block_send, recv_sem=block_recv,
            device_id=(section, row, c), device_id_type=MESH,
        ).start()
        return carry

    lax.fori_loop(1, n_col, send_block, 0)

    arrived = factors.reshape(2 * k_tiles * size, LANES)
    strip = 256

    def product_step(first, kt, carry):
        wait_for(factors.at[:, kt], factor_recv.at[kt])
        right = arrived[pl.ds(pl.multiple_of((k_tiles + kt) * size, size), size), :]
        for m in range(0, size, strip):
            left = arrived[pl.ds(pl.multiple_of(kt * size + m, strip), strip), :]
            part = lax.dot_general(left, right, (((1,), (1,)), ((), ())), preferred_element_type=F32)
            products[m : m + strip, :] = part if first else products[m : m + strip, :] + part
        return carry

    product_step(True, 0, 0)
    lax.fori_loop(1, 3, functools.partial(product_step, False), 0)

    wait_for(block, block_recv)

    def gate_step(i, carry):
        normed = norm(block[i].astype(F32), g_in[...], 1)
        gate[i] = jax.nn.sigmoid(
            jnp.dot(normed, w_in[0, :, 4 * hidden :], preferred_element_type=F32)
        )
        return carry

    lax.fori_loop(0, row_count, gate_step, 0)
    lax.fori_loop(3, k_tiles, functools.partial(product_step, False), 0)

    kept = parts * part_rows
    product_rows = product_out.reshape(parts * devices * part_rows, LANES)
    spare = LANES - col_count

    for part in range(parts):

        def pack(d, carry, part=part):
            r = lax.rem(row + d, n_row)
            tile_rows = products[pl.ds(pl.multiple_of(r * row_count, row_count), row_count), :]
            for c in range(n_col):
                into = slice(c * part_rows, (c + 1) * part_rows)
                packed_f32[into, :col_count] = tile_rows[
                    part * part_rows : (part + 1) * part_rows, c * col_count : (c + 1) * col_count
                ]
                begin = c * col_count + part * spare
                packed_f32[into, col_count:] = tile_rows[kept:, begin : begin + spare]
            base = part * devices + r * n_col
            product_rows[pl.ds(pl.multiple_of(base * part_rows, n_col * part_rows), n_col * part_rows), :] = (
                packed_f32[...].astype(BF16)
            )

            def send(e, cc):
                c = lax.rem(col + e, n_col)
                t = r * n_col + c

                @pl.when(t != me)
                def _():
                    pltpu.make_async_remote_copy(
                        src_ref=product_out.at[part, t], dst_ref=product_in.at[part, me],
                        send_sem=product_send, recv_sem=product_recv.at[part],
                        device_id=(section, r, c), device_id_type=MESH,
                    ).start()

                @pl.when(t == me)
                def _():
                    pltpu.make_async_copy(
                        product_out.at[part, me], product_in.at[part, me], product_recv.at[part]
                    ).start()

                return cc

            lax.fori_loop(0, n_col, send, 0)
            return carry

        lax.fori_loop(0, n_row, pack, 0)

    product_in_rows = product_in.reshape(parts * devices * part_rows, LANES)
    for part in range(parts):
        wait_for(product_in.at[part], product_recv.at[part])
        product_f32[...] = product_in_rows[
            part * devices * part_rows : (part + 1) * devices * part_rows, :
        ].astype(F32)

        def finish(q, carry, part=part):
            normed = norm(product_f32[pl.ds(q, devices, stride=part_rows), :], g_cols[...], 0)
            update = lax.dot_general(
                normed, w_out[0], (((0,), (0,)), ((), ())), preferred_element_type=F32
            )
            i = part * part_rows + q
            out[0, i] = (block[i].astype(F32) + gate[i] * update[:col_count]).astype(BF16)
            i, j = kept + q, slice(part * spare, (part + 1) * spare)
            out[0, i, j] = (block[i, j].astype(F32) + gate[i, j] * update[col_count:]).astype(BF16)
            return carry

        lax.fori_loop(0, part_rows, finish, 0)

    wait_for(slab, slab_send)
    wait_for(factor_out.at[:, pl.ds(0, devices - 1)], factor_send)
    wait_for(product_out.at[:, pl.ds(0, devices - 1)], product_send)
    wait_for(block.at[pl.ds(0, (n_col - 1) * rows)], block_send)


def local(n_row, n_col, handed, residue_mask, input_weights, input_gain, product_gain, output_weights):
    _, rows, size, channels = handed.shape
    hidden = output_weights.shape[1]
    devices = n_row * n_col
    k_tiles = size // LANES
    row_count, col_count = size // n_row, size // n_col
    message = row_count * col_count // LANES
    parts = 3
    part_rows = message // parts
    vmem = pl.BlockSpec(memory_space=pltpu.VMEM)
    dma = pltpu.SemaphoreType.DMA
    return pl.pallas_call(
        functools.partial(kernel, n_row, n_col),
        out_shape=jax.ShapeDtypeStruct((1, row_count, col_count, channels), BF16),
        in_specs=[pl.BlockSpec(memory_space=pl.ANY)] + [vmem] * 5,
        out_specs=vmem,
        scratch_shapes=[
            pltpu.VMEM((rows, size, channels), BF16),
            pltpu.VMEM((1, size), jnp.int32),
            pltpu.VMEM(input_weights.shape[:0:-1], BF16),
            pltpu.VMEM((hidden, LANES), F32),
            pltpu.VMEM((devices * 2 * rows, LANES), F32),
            pltpu.VMEM((k_tiles, devices, 2, rows // 2, 2, LANES), BF16),
            pltpu.VMEM((2, k_tiles, size // 2, 2, LANES), BF16),
            pltpu.VMEM((size, size), F32),
            pltpu.VMEM((n_col * part_rows, LANES), F32),
            pltpu.VMEM((parts, devices, part_rows // 2, 2, LANES), BF16),
            pltpu.VMEM((parts, devices, part_rows // 2, 2, LANES), BF16),
            pltpu.VMEM((devices * part_rows, LANES), F32),
            pltpu.VMEM((row_count, col_count, channels), BF16),
            pltpu.VMEM((row_count, col_count, channels), F32),
            dma((2,)), dma, dma((k_tiles,)), dma, dma((k_tiles,)),
            dma, dma((parts,)), dma, dma,
        ],
        compiler_params=pltpu.CompilerParams(
            collective_id=0, has_side_effects=True, vmem_limit_bytes=48 * 2**20
        ),
    )(handed, residue_mask, input_weights, input_gain, product_gain, output_weights)


def solution(mesh):
    placed = (
        P("section", ("row", "col"), None, None),
        P("section", None),
        P("section", None, None),
        P("section", None),
        P("section", None),
        P("section", None, None),
    )
    return jax.shard_map(
        functools.partial(local, mesh.shape["row"], mesh.shape["col"]),
        mesh=mesh,
        in_specs=placed,
        out_specs=P("section", "row", "col", None),
        check_vma=False,
    )
```

```python
import functools

import jax
import jax.numpy as jnp
from jax import lax
from jax.experimental import pallas as pl
from jax.experimental.pallas import tpu as pltpu
from jax.sharding import PartitionSpec as P

EPS = 1e-05
LANES = 128
MESH = pl.DeviceIdType.MESH
BF16 = jnp.bfloat16
F32 = jnp.float32


def norm(values, gain, axis):
    center = jnp.mean(values, axis=axis, keepdims=True)
    deviate = values - center
    spread = jnp.mean(deviate * deviate, axis=axis, keepdims=True)
    return (deviate * lax.rsqrt(spread + EPS) * gain).astype(BF16)


def wait_for(ref, sem):
    pltpu.make_async_copy(ref, ref, sem).wait()


def kernel(
    n_row, n_col,
    handed, mask, w_in_hbm, g_in_hbm, g_prod_hbm, w_out_hbm, out,
    w_in, g_in, g_prod, w_out, slab, flags, w_cols, g_cols, factor_f32, factor_out, factors, products,
    packed_f32, product_out, product_in, product_f32, block, gate,
    load_sems, flag_sems, slab_send, slab_recv, factor_send, factor_recv,
    product_send, product_recv, block_send, block_recv,
):
    rows, size, channels = slab.shape
    hidden = w_out.shape[1]
    k_tiles = size // LANES
    devices = n_row * n_col
    row_count, col_count = size // n_row, size // n_col
    parts, _, part_rows = product_out.shape[0], 0, 2 * product_out.shape[2]
    section, row, col = (lax.axis_index(a) for a in ("section", "row", "col"))
    me = row * n_col + col
    partner = (1 - section, row, col)

    def at(t):
        return (section, t // n_col, lax.rem(t, n_col))

    loads = [
        pltpu.make_async_copy(source, target, load_sems.at[i])
        for i, (source, target) in enumerate(
            ((w_in_hbm, w_in), (g_prod_hbm, g_prod), (g_in_hbm, g_in), (w_out_hbm, w_out))
        )
    ]
    for load in loads:
        load.start()
    barrier = pltpu.get_barrier_semaphore()
    pl.semaphore_signal(barrier, inc=1, device_id=partner, device_id_type=MESH)

    def greet(d, carry):
        pl.semaphore_signal(barrier, inc=1, device_id=at(lax.rem(me + d, devices)), device_id_type=MESH)
        return carry

    lax.fori_loop(1, devices, greet, 0)
    for load in loads:
        load.wait()
    w_cols[...] = w_in[0].astype(F32).T.astype(BF16)
    g_cols[...] = jnp.broadcast_to(g_prod[...], (LANES, hidden)).T
    pl.semaphore_wait(barrier, devices)

    flag_copy = pltpu.make_async_remote_copy(
        src_ref=mask, dst_ref=flags, send_sem=flag_sems.at[0], recv_sem=flag_sems.at[1],
        device_id=partner, device_id_type=MESH,
    )
    flag_copy.start()

    def tile(kt):
        return pl.ds(pl.multiple_of(kt * LANES, LANES), LANES)

    def slab_copy(kt):
        return pltpu.make_async_remote_copy(
            src_ref=handed.at[0, :, tile(kt)], dst_ref=slab.at[:, tile(kt)],
            send_sem=slab_send, recv_sem=slab_recv.at[kt],
            device_id=partner, device_id_type=MESH,
        )

    slab_copy(0).start()
    slab_copy(1).start()
    flag_copy.wait()

    def columns(c):
        return pl.ds(pl.multiple_of(c * col_count, col_count), col_count)

    block_rows = block.at[pl.ds(col * rows, rows)]

    def send_block(c, carry):
        @pl.when(c != col)
        def _():
            pltpu.make_async_remote_copy(
                src_ref=slab.at[:, columns(c)], dst_ref=block_rows,
                send_sem=block_send, recv_sem=block_recv,
                device_id=(section, row, c), device_id_type=MESH,
            ).start()

        @pl.when(c == col)
        def _():
            pltpu.make_async_copy(slab.at[:, columns(c)], block_rows, block_recv).start()

        return carry

    per_owner = 2 * rows
    factor_rows = factor_out.reshape(k_tiles * devices * per_owner, LANES)
    all_flags = flags[...].astype(F32)
    places = lax.broadcasted_iota(jnp.int32, all_flags.shape, 1)
    own_flags = [
        jnp.sum(jnp.where(places == me * rows + i, all_flags, 0.0), axis=1, keepdims=True)
        for i in range(rows)
    ]

    def factor_step(kt, carry):
        wait_for(slab.at[:, tile(kt)], slab_recv.at[kt])

        @pl.when(kt + 2 < k_tiles)
        def _():
            slab_copy(kt + 2).start()

        k_flags = flags[:, tile(kt)].astype(F32)
        for i in range(rows):
            normed = norm(slab[i, tile(kt), :].astype(F32), g_in[...], 1)
            projected = lax.dot_general(
                w_cols[: 4 * hidden], normed, (((1,), (1,)), ((), ())), preferred_element_type=F32
            )
            pair_flags = k_flags * own_flags[i]
            for side in range(2):
                gates = projected[2 * side * hidden : (2 * side + 1) * hidden]
                values = projected[(2 * side + 1) * hidden : (2 * side + 2) * hidden]
                factor_f32[pl.ds(side * rows + i, hidden, stride=per_owner), :] = (
                    jax.nn.sigmoid(gates) * values * pair_flags
                )
        begin = pl.multiple_of(kt * (devices * per_owner), devices * per_owner)
        factor_rows[pl.ds(begin, devices * per_owner), :] = factor_f32[...].astype(BF16)
        target = factors.at[:, kt, pl.ds(me * (rows // 2), rows // 2)]
        pltpu.make_async_copy(factor_out.at[kt, me], target, factor_recv.at[kt]).start()

        def send(d, c):
            t = lax.rem(me + d, devices)
            pltpu.make_async_remote_copy(
                src_ref=factor_out.at[kt, t], dst_ref=target,
                send_sem=factor_send, recv_sem=factor_recv.at[kt],
                device_id=at(t), device_id_type=MESH,
            ).start()
            return c

        lax.fori_loop(1, devices, send, 0)
        return carry

    lax.fori_loop(0, k_tiles, factor_step, 0)

    def send_block_turn(d, carry):
        return send_block(lax.rem(col + d, n_col), carry)

    lax.fori_loop(0, n_col, send_block_turn, 0)

    arrived = factors.reshape(2 * k_tiles * size, LANES)
    strip = 256

    def product_step(first, kt, carry):
        wait_for(factors.at[:, kt], factor_recv.at[kt])
        right = arrived[pl.ds(pl.multiple_of((k_tiles + kt) * size, size), size), :]
        for m in range(0, size, strip):
            left = arrived[pl.ds(pl.multiple_of(kt * size + m, strip), strip), :]
            part = lax.dot_general(left, right, (((1,), (1,)), ((), ())), preferred_element_type=F32)
            products[m : m + strip, :] = part if first else products[m : m + strip, :] + part
        return carry

    product_step(True, 0, 0)
    lax.fori_loop(1, k_tiles, functools.partial(product_step, False), 0)

    kept = parts * part_rows
    product_rows = product_out.reshape(parts * devices * part_rows, LANES)
    spare = LANES - col_count

    for part in range(parts):

        def pack(d, carry, part=part):
            r = lax.rem(row + d, n_row)
            tile_rows = products[pl.ds(pl.multiple_of(r * row_count, row_count), row_count), :]
            for c in range(n_col):
                into = slice(c * part_rows, (c + 1) * part_rows)
                packed_f32[into, :col_count] = tile_rows[
                    part * part_rows : (part + 1) * part_rows, c * col_count : (c + 1) * col_count
                ]
                begin = c * col_count + part * spare
                packed_f32[into, col_count:] = tile_rows[kept:, begin : begin + spare]
            base = part * devices + r * n_col
            product_rows[pl.ds(pl.multiple_of(base * part_rows, n_col * part_rows), n_col * part_rows), :] = (
                packed_f32[...].astype(BF16)
            )

            def send(e, cc):
                c = lax.rem(col + e, n_col)
                t = r * n_col + c

                @pl.when(t != me)
                def _():
                    pltpu.make_async_remote_copy(
                        src_ref=product_out.at[part, t], dst_ref=product_in.at[part, me],
                        send_sem=product_send, recv_sem=product_recv.at[part],
                        device_id=(section, r, c), device_id_type=MESH,
                    ).start()

                @pl.when(t == me)
                def _():
                    pltpu.make_async_copy(
                        product_out.at[part, me], product_in.at[part, me], product_recv.at[part]
                    ).start()

                return cc

            lax.fori_loop(0, n_col, send, 0)
            return carry

        lax.fori_loop(0, n_row, pack, 0)

    wait_for(block, block_recv)

    batch = 4

    def gate_step(b, carry):
        some = pl.ds(b * batch, batch)
        flat = block[some].reshape(batch * col_count, channels)
        normed = norm(flat.astype(F32), g_in[...], 1)
        gating = jnp.dot(normed, w_in[0, :, 4 * hidden :], preferred_element_type=F32)
        gate[some] = jax.nn.sigmoid(gating).reshape(batch, col_count, channels)
        return carry

    lax.fori_loop(0, row_count // batch, gate_step, 0)
    product_in_rows = product_in.reshape(parts * devices * part_rows, LANES)
    for part in range(parts):
        wait_for(product_in.at[part], product_recv.at[part])
        product_f32[...] = product_in_rows[
            part * devices * part_rows : (part + 1) * devices * part_rows, :
        ].astype(F32)

        def finish(q, carry, part=part):
            normed = norm(product_f32[pl.ds(q, devices, stride=part_rows), :], g_cols[...], 0)
            update = lax.dot_general(
                normed, w_out[0], (((0,), (0,)), ((), ())), preferred_element_type=F32
            )
            i = part * part_rows + q
            out[0, i] = (block[i].astype(F32) + gate[i] * update[:col_count]).astype(BF16)
            i, j = kept + q, slice(part * spare, (part + 1) * spare)
            out[0, i, j] = (block[i, j].astype(F32) + gate[i, j] * update[col_count:]).astype(BF16)
            return carry

        lax.fori_loop(0, part_rows, finish, 0)

    wait_for(slab, slab_send)
    wait_for(factor_out.at[:, pl.ds(0, devices - 1)], factor_send)
    wait_for(product_out.at[:, pl.ds(0, devices - 1)], product_send)
    wait_for(block.at[pl.ds(0, (n_col - 1) * rows)], block_send)


def local(n_row, n_col, handed, residue_mask, input_weights, input_gain, product_gain, output_weights):
    _, rows, size, channels = handed.shape
    hidden = output_weights.shape[1]
    devices = n_row * n_col
    k_tiles = size // LANES
    row_count, col_count = size // n_row, size // n_col
    message = row_count * col_count // LANES
    parts = 3
    part_rows = message // parts
    vmem = pl.BlockSpec(memory_space=pltpu.VMEM)
    dma = pltpu.SemaphoreType.DMA
    return pl.pallas_call(
        functools.partial(kernel, n_row, n_col),
        out_shape=jax.ShapeDtypeStruct((1, row_count, col_count, channels), BF16),
        in_specs=[pl.BlockSpec(memory_space=pl.ANY)] * 6,
        out_specs=vmem,
        scratch_shapes=[
            pltpu.VMEM(input_weights.shape, BF16),
            pltpu.VMEM(input_gain.shape, F32),
            pltpu.VMEM(product_gain.shape, F32),
            pltpu.VMEM(output_weights.shape, BF16),
            pltpu.VMEM((rows, size, channels), BF16),
            pltpu.VMEM((1, size), jnp.int32),
            pltpu.VMEM(input_weights.shape[:0:-1], BF16),
            pltpu.VMEM((hidden, LANES), F32),
            pltpu.VMEM((devices * 2 * rows, LANES), F32),
            pltpu.VMEM((k_tiles, devices, 2, rows // 2, 2, LANES), BF16),
            pltpu.VMEM((2, k_tiles, size // 2, 2, LANES), BF16),
            pltpu.VMEM((size, size), F32),
            pltpu.VMEM((n_col * part_rows, LANES), F32),
            pltpu.VMEM((parts, devices, part_rows // 2, 2, LANES), BF16),
            pltpu.VMEM((parts, devices, part_rows // 2, 2, LANES), BF16),
            pltpu.VMEM((devices * part_rows, LANES), F32),
            pltpu.VMEM((row_count, col_count, channels), BF16),
            pltpu.VMEM((row_count, col_count, channels), F32),
            dma((4,)), dma((2,)), dma, dma((k_tiles,)), dma, dma((k_tiles,)),
            dma, dma((parts,)), dma, dma,
        ],
        compiler_params=pltpu.CompilerParams(
            collective_id=0, has_side_effects=True, vmem_limit_bytes=48 * 2**20
        ),
    )(handed, residue_mask, input_weights, input_gain, product_gain, output_weights)


def solution(mesh):
    placed = (
        P("section", ("row", "col"), None, None),
        P("section", None),
        P("section", None, None),
        P("section", None),
        P("section", None),
        P("section", None, None),
    )
    return jax.shard_map(
        functools.partial(local, mesh.shape["row"], mesh.shape["col"]),
        mesh=mesh,
        in_specs=placed,
        out_specs=P("section", "row", "col", None),
        check_vma=False,
    )
```

```python
import functools

import jax
import jax.numpy as jnp
from jax import lax
from jax.experimental import pallas as pl
from jax.experimental.pallas import tpu as pltpu
from jax.sharding import PartitionSpec as P

EPS = 1e-05
LANES = 128
MESH = pl.DeviceIdType.MESH
BF16 = jnp.bfloat16
F32 = jnp.float32


def norm(values, gain, axis):
    center = jnp.mean(values, axis=axis, keepdims=True)
    deviate = values - center
    spread = jnp.mean(deviate * deviate, axis=axis, keepdims=True)
    return (deviate * lax.rsqrt(spread + EPS) * gain).astype(BF16)


def wait_for(ref, sem):
    pltpu.make_async_copy(ref, ref, sem).wait()


def kernel(
    n_row, n_col,
    handed, mask, w_in_hbm, g_in_hbm, g_prod_hbm, w_out_hbm, out,
    w_in, g_in, g_prod, w_out, slab, flags, w_cols, g_cols, factor_f32, factor_out, factors, products,
    packed_f32, product_out, product_in, product_f32, block, gate,
    load_sems, flag_sems, slab_send, slab_recv, factor_send, factor_recv, twin_send, twin_recv,
    product_send, product_recv, block_send, block_recv,
):
    rows, size, channels = slab.shape
    hidden = w_out.shape[1]
    k_tiles = size // LANES
    devices = n_row * n_col
    row_count, col_count = size // n_row, size // n_col
    parts, part_rows = product_out.shape[0], 2 * product_out.shape[2]
    section, row, col = (lax.axis_index(a) for a in ("section", "row", "col"))
    me = row * n_col + col

    ring = n_row // 2
    half = ring // 2
    plane, side_y, core = row // 2, lax.rem(row, 2), lax.rem(col, 2)

    held_row = plane * 2 + 1 - side_y
    partner = (1 - section, held_row, col)

    def pair_base(z, c):
        return lax.rem(lax.rem(z - c + ring, ring) // 2 * 2 + c, ring)

    base = pair_base(plane, core)
    upper = lax.rem(plane - base + ring, ring)
    first_plane = lax.rem(base + half * upper + ring + 1 - half, ring)
    twin = (section, lax.rem(base + 1 - upper, ring) * 2 + side_y, col)
    own_channels = [(lax.rem(base + i, ring) * 2 + side_y) * n_col + col for i in range(2)]

    loads = [
        pltpu.make_async_copy(source, target, load_sems.at[i])
        for i, (source, target) in enumerate(
            ((w_in_hbm, w_in), (g_prod_hbm, g_prod), (g_in_hbm, g_in), (w_out_hbm, w_out))
        )
    ]
    for load in loads:
        load.start()
    barrier = pltpu.get_barrier_semaphore()
    pl.semaphore_signal(barrier, inc=1, device_id=partner, device_id_type=MESH)

    def greet(d, carry):
        for e in range(n_col):
            r, c = lax.rem(row + d, n_row), lax.rem(col + e, n_col)

            @pl.when((d > 0) | (e > 0))
            def _():
                pl.semaphore_signal(barrier, inc=1, device_id=(section, r, c), device_id_type=MESH)

        return carry

    lax.fori_loop(0, n_row, greet, 0)
    for load in loads:
        load.wait()
    w_cols[...] = w_in[0].astype(F32).T.astype(BF16)
    g_cols[...] = jnp.broadcast_to(g_prod[...], (LANES, hidden)).T
    pl.semaphore_wait(barrier, devices)

    flag_copy = pltpu.make_async_remote_copy(
        src_ref=mask, dst_ref=flags, send_sem=flag_sems.at[0], recv_sem=flag_sems.at[1],
        device_id=partner, device_id_type=MESH,
    )
    flag_copy.start()

    def tile(kt):
        return pl.ds(pl.multiple_of(kt * LANES, LANES), LANES)

    def slab_copy(kt):
        return pltpu.make_async_remote_copy(
            src_ref=handed.at[0, :, tile(kt)], dst_ref=slab.at[:, tile(kt)],
            send_sem=slab_send, recv_sem=slab_recv.at[kt],
            device_id=partner, device_id_type=MESH,
        )

    slab_copy(0).start()
    slab_copy(1).start()
    flag_copy.wait()

    def columns(c):
        return pl.ds(pl.multiple_of(c * col_count, col_count), col_count)

    block_rows = block.at[pl.ds(col * rows, rows)]

    def send_block(d, carry):
        c = lax.rem(col + d, n_col)
        pltpu.make_async_remote_copy(
            src_ref=slab.at[:, columns(c)], dst_ref=block_rows,
            send_sem=block_send, recv_sem=block_recv,
            device_id=(section, held_row, c), device_id_type=MESH,
        ).start()
        return carry

    per_owner = 2 * rows
    factor_rows = factor_out.reshape(k_tiles * devices * per_owner, LANES)
    all_flags = flags[...].astype(F32)
    places = lax.broadcasted_iota(jnp.int32, all_flags.shape, 1)
    own_flags = [
        jnp.sum(jnp.where(places == (held_row * n_col + col) * rows + i, all_flags, 0.0), axis=1, keepdims=True)
        for i in range(rows)
    ]

    def factor_step(kt, carry):
        wait_for(slab.at[:, tile(kt)], slab_recv.at[kt])

        @pl.when(kt + 2 < k_tiles)
        def _():
            slab_copy(kt + 2).start()

        k_flags = flags[:, tile(kt)].astype(F32)
        for i in range(rows):
            normed = norm(slab[i, tile(kt), :].astype(F32), g_in[...], 1)
            projected = lax.dot_general(
                w_cols[: 4 * hidden], normed, (((1,), (1,)), ((), ())), preferred_element_type=F32
            )
            pair_flags = k_flags * own_flags[i]
            for side in range(2):
                gates = projected[2 * side * hidden : (2 * side + 1) * hidden]
                values = projected[(2 * side + 1) * hidden : (2 * side + 2) * hidden]
                factor_f32[pl.ds(side * rows + i, hidden, stride=per_owner), :] = (
                    jax.nn.sigmoid(gates) * values * pair_flags
                )
        begin = pl.multiple_of(kt * (devices * per_owner), devices * per_owner)
        factor_rows[pl.ds(begin, devices * per_owner), :] = factor_f32[...].astype(BF16)

        def send(d, c):
            r = lax.rem(row + d, n_row)
            for parity in range(2):
                z = r // 2
                low = pair_base(z, lax.rem(core + parity, 2))
                turn = lax.rem(plane - low + half - 1 + ring, ring)
                near = lax.rem(low + turn // half, ring) * 2 + lax.rem(r, 2)
                place = (lax.rem(turn, half) * 2 + 1 - side_y) * n_col + col
                target = factors.at[
                    pl.ds(0, 2), lax.rem(z - low + ring, ring), kt, pl.ds(place * (rows // 2), rows // 2)
                ]
                for e in range(parity, n_col, 2):
                    channel_col = lax.rem(col + e, n_col)
                    source = factor_out.at[kt, r * n_col + channel_col]

                    def remote(source=source, target=target, near=near, channel_col=channel_col):
                        pltpu.make_async_remote_copy(
                            src_ref=source, dst_ref=target,
                            send_sem=factor_send, recv_sem=factor_recv.at[kt],
                            device_id=(section, near, channel_col), device_id_type=MESH,
                        ).start()

                    if e:
                        remote()
                    else:
                        pl.when(near != row)(remote)

                        @pl.when(near == row)
                        def _(source=source, target=target):
                            pltpu.make_async_copy(source, target, factor_recv.at[kt]).start()

            return c

        lax.fori_loop(0, n_row, send, 0)
        return carry

    lax.fori_loop(0, k_tiles, factor_step, 0)

    lax.fori_loop(0, n_col, send_block, 0)

    span = size // 2
    arrived = factors.reshape(3 * 2 * k_tiles * span, LANES)

    def product_step(first, which, kt):
        for channel in range(2):
            def operand(kind):
                begin = ((kind * 2 + channel) * k_tiles + kt) * span
                return arrived[pl.ds(pl.multiple_of(begin, span), span), :]

            part = lax.dot_general(
                operand(0), operand(1 + which), (((1,), (1,)), ((), ())), preferred_element_type=F32
            )
            spot = (slice(channel * span, (channel + 1) * span), slice(which * span, (which + 1) * span))
            products[spot] = part if first else products[spot] + part

    def twin_copy(kt):
        return pltpu.make_async_remote_copy(
            src_ref=factors.at[1, :, kt], dst_ref=factors.at[2, :, kt],
            send_sem=twin_send, recv_sem=twin_recv.at[kt],
            device_id=twin, device_id_type=MESH,
        )

    def take(kt):
        wait_for(factors.at[pl.ds(0, 2), :, kt], factor_recv.at[kt])
        twin_copy(kt).start()

    def take_twin(kt):
        wait_for(factors.at[2, :, kt], twin_recv.at[kt])

    def product_steps(kt, carry):
        take(kt)
        product_step(False, 0, kt)
        take_twin(kt - 1)
        product_step(False, 1, kt - 1)
        return carry

    take(0)
    product_step(True, 0, 0)
    take(1)
    product_step(False, 0, 1)
    take_twin(0)
    product_step(True, 1, 0)
    lax.fori_loop(2, k_tiles, product_steps, 0)

    kept = parts * part_rows
    product_rows = product_out.reshape(parts * devices * part_rows, LANES)
    spare = LANES - col_count

    def pack(part, begin_block, end_block):
        blocks = end_block - begin_block

        def step(d, carry):
            channel, group = lax.rem(d, 2), d // 2
            tile_rows = products[
                pl.ds(pl.multiple_of(channel * span + group * row_count, row_count), row_count),
                begin_block * col_count : end_block * col_count,
            ]
            for c in range(blocks):
                into = slice(c * part_rows, (c + 1) * part_rows)
                packed_f32[into, :col_count] = tile_rows[
                    part * part_rows : (part + 1) * part_rows, c * col_count : (c + 1) * col_count
                ]
                begin = c * col_count + part * spare
                packed_f32[into, col_count:] = tile_rows[kept:, begin : begin + spare]
            index = (channel * n_col + group) * n_col + begin_block
            begin = (part * devices + index) * part_rows
            product_rows[pl.ds(pl.multiple_of(begin, 4 * part_rows), blocks * part_rows), :] = (
                packed_f32[: blocks * part_rows, :].astype(BF16)
            )
            r = lax.rem(first_plane + group // 2, ring) * 2 + lax.rem(group, 2)
            own = own_channels[0] + channel * (own_channels[1] - own_channels[0])
            for m in range(begin_block, end_block):
                c = lax.rem(first_plane + m, n_col)
                source = product_out.at[part, index + (m - begin_block)]
                target = product_in.at[part, own]
                here = (r == row) & (c == col)

                @pl.when(jnp.logical_not(here))
                def _(source=source, target=target, c=c):
                    pltpu.make_async_remote_copy(
                        src_ref=source, dst_ref=target,
                        send_sem=product_send, recv_sem=product_recv.at[part],
                        device_id=(section, r, c), device_id_type=MESH,
                    ).start()

                @pl.when(here)
                def _(source=source, target=target):
                    pltpu.make_async_copy(source, target, product_recv.at[part]).start()

            return carry

        lax.fori_loop(0, n_row, step, 0)

    pack(0, 0, n_col // 2)
    take_twin(k_tiles - 1)
    product_step(False, 1, k_tiles - 1)
    pack(0, n_col // 2, n_col)
    for part in range(1, parts):
        pack(part, 0, n_col)

    wait_for(block, block_recv)

    batch = 4

    def gate_step(b, carry):
        some = pl.ds(b * batch, batch)
        flat = block[some].reshape(batch * col_count, channels)
        normed = norm(flat.astype(F32), g_in[...], 1)
        gating = jnp.dot(normed, w_in[0, :, 4 * hidden :], preferred_element_type=F32)
        gate[some] = jax.nn.sigmoid(gating).reshape(batch, col_count, channels)
        return carry

    lax.fori_loop(0, row_count // batch, gate_step, 0)
    product_in_rows = product_in.reshape(parts * devices * part_rows, LANES)
    for part in range(parts):
        wait_for(product_in.at[part], product_recv.at[part])
        product_f32[...] = product_in_rows[
            part * devices * part_rows : (part + 1) * devices * part_rows, :
        ].astype(F32)

        def finish(q, carry, part=part):
            normed = norm(product_f32[pl.ds(q, devices, stride=part_rows), :], g_cols[...], 0)
            update = lax.dot_general(
                normed, w_out[0], (((0,), (0,)), ((), ())), preferred_element_type=F32
            )
            i = part * part_rows + q
            out[0, i] = (block[i].astype(F32) + gate[i] * update[:col_count]).astype(BF16)
            i, j = kept + q, slice(part * spare, (part + 1) * spare)
            out[0, i, j] = (block[i, j].astype(F32) + gate[i, j] * update[col_count:]).astype(BF16)
            return carry

        lax.fori_loop(0, part_rows, finish, 0)

    wait_for(slab, slab_send)
    wait_for(factor_out.at[:, pl.ds(0, devices - 2)], factor_send)
    wait_for(factors.at[1], twin_send)
    wait_for(product_out.at[:, pl.ds(0, devices - 2)], product_send)
    wait_for(block, block_send)


def local(n_row, n_col, handed, residue_mask, input_weights, input_gain, product_gain, output_weights):
    _, rows, size, channels = handed.shape
    hidden = output_weights.shape[1]
    devices = n_row * n_col
    k_tiles = size // LANES
    row_count, col_count = size // n_row, size // n_col
    message = row_count * col_count // LANES
    parts = 3
    part_rows = message // parts
    vmem = pl.BlockSpec(memory_space=pltpu.VMEM)
    dma = pltpu.SemaphoreType.DMA
    return pl.pallas_call(
        functools.partial(kernel, n_row, n_col),
        out_shape=jax.ShapeDtypeStruct((1, row_count, col_count, channels), BF16),
        in_specs=[pl.BlockSpec(memory_space=pl.ANY)] * 6,
        out_specs=vmem,
        scratch_shapes=[
            pltpu.VMEM(input_weights.shape, BF16),
            pltpu.VMEM(input_gain.shape, F32),
            pltpu.VMEM(product_gain.shape, F32),
            pltpu.VMEM(output_weights.shape, BF16),
            pltpu.VMEM((rows, size, channels), BF16),
            pltpu.VMEM((1, size), jnp.int32),
            pltpu.VMEM(input_weights.shape[:0:-1], BF16),
            pltpu.VMEM((hidden, LANES), F32),
            pltpu.VMEM((devices * 2 * rows, LANES), F32),
            pltpu.VMEM((k_tiles, devices, 2, rows // 2, 2, LANES), BF16),
            pltpu.VMEM((3, 2, k_tiles, size // 4, 2, LANES), BF16),
            pltpu.VMEM((size, size), F32),
            pltpu.VMEM((n_col * part_rows, LANES), F32),
            pltpu.VMEM((parts, devices, part_rows // 2, 2, LANES), BF16),
            pltpu.VMEM((parts, devices, part_rows // 2, 2, LANES), BF16),
            pltpu.VMEM((devices * part_rows, LANES), F32),
            pltpu.VMEM((row_count, col_count, channels), BF16),
            pltpu.VMEM((row_count, col_count, channels), F32),
            dma((4,)), dma((2,)), dma, dma((k_tiles,)), dma, dma((k_tiles,)),
            dma, dma((k_tiles,)), dma, dma((parts,)), dma, dma,
        ],
        compiler_params=pltpu.CompilerParams(
            collective_id=0, has_side_effects=True, vmem_limit_bytes=48 * 2**20
        ),
    )(handed, residue_mask, input_weights, input_gain, product_gain, output_weights)


def solution(mesh):
    placed = (
        P("section", ("row", "col"), None, None),
        P("section", None),
        P("section", None, None),
        P("section", None),
        P("section", None),
        P("section", None, None),
    )
    return jax.shard_map(
        functools.partial(local, mesh.shape["row"], mesh.shape["col"]),
        mesh=mesh,
        in_specs=placed,
        out_specs=P("section", "row", "col", None),
        check_vma=False,
    )
```

```python
import functools

import jax
import jax.numpy as jnp
from jax import lax
from jax.experimental import pallas as pl
from jax.experimental.pallas import tpu as pltpu
from jax.sharding import PartitionSpec as P

EPS = 1e-05
LANES = 128
MESH = pl.DeviceIdType.MESH
BF16 = jnp.bfloat16
F32 = jnp.float32


def norm(values, gain, axis):
    center = jnp.mean(values, axis=axis, keepdims=True)
    deviate = values - center
    spread = jnp.mean(deviate * deviate, axis=axis, keepdims=True)
    return (deviate * lax.rsqrt(spread + EPS) * gain).astype(BF16)


def wait_for(ref, sem):
    pltpu.make_async_copy(ref, ref, sem).wait()


def kernel(
    n_row, n_col,
    handed, mask, w_in_hbm, g_in_hbm, g_prod_hbm, w_out_hbm, out,
    w_in, g_in, g_prod, w_out, slab, flags, w_cols, g_cols, factor_f32, factor_out, factors, products,
    packed_f32, product_out, product_in, product_f32, block, gate,
    load_sems, flag_sems, slab_send, slab_recv, factor_send, factor_recv, twin_send, twin_recv,
    product_send, product_recv, block_send, block_recv,
):
    rows, size, channels = slab.shape
    hidden = w_out.shape[1]
    k_tiles = size // LANES
    devices = n_row * n_col
    row_count, col_count = size // n_row, size // n_col
    parts, part_rows = product_out.shape[0], 2 * product_out.shape[2]
    section, row, col = (lax.axis_index(a) for a in ("section", "row", "col"))
    me = row * n_col + col

    ring = n_row // 2
    half = ring // 2
    plane, side_y, core = row // 2, lax.rem(row, 2), lax.rem(col, 2)

    held_row = plane * 2 + 1 - side_y
    partner = (1 - section, held_row, col)

    def pair_base(z, c):
        return lax.rem(lax.rem(z - c + ring, ring) // 2 * 2 + c, ring)

    base = pair_base(plane, core)
    upper = lax.rem(plane - base + ring, ring)
    first_plane = lax.rem(base + half * upper + ring + 1 - half, ring)
    twin = (section, lax.rem(base + 1 - upper, ring) * 2 + side_y, col)
    own_channels = [(lax.rem(base + i, ring) * 2 + side_y) * n_col + col for i in range(2)]

    loads = [
        pltpu.make_async_copy(source, target, load_sems.at[i])
        for i, (source, target) in enumerate(
            ((w_in_hbm, w_in), (g_prod_hbm, g_prod), (g_in_hbm, g_in), (w_out_hbm, w_out))
        )
    ]
    for load in loads:
        load.start()
    barrier = pltpu.get_barrier_semaphore()
    pl.semaphore_signal(barrier, inc=1, device_id=partner, device_id_type=MESH)

    def greet(d, carry):
        for e in range(n_col):
            r, c = lax.rem(row + d, n_row), lax.rem(col + e, n_col)

            @pl.when((d > 0) | (e > 0))
            def _():
                pl.semaphore_signal(barrier, inc=1, device_id=(section, r, c), device_id_type=MESH)

        return carry

    lax.fori_loop(0, n_row, greet, 0)
    for load in loads:
        load.wait()
    w_cols[...] = w_in[0].astype(F32).T.astype(BF16)
    g_cols[...] = jnp.broadcast_to(g_prod[...], (LANES, hidden)).T
    pl.semaphore_wait(barrier, devices)

    flag_copy = pltpu.make_async_remote_copy(
        src_ref=mask, dst_ref=flags, send_sem=flag_sems.at[0], recv_sem=flag_sems.at[1],
        device_id=partner, device_id_type=MESH,
    )
    flag_copy.start()

    def tile(kt):
        return pl.ds(pl.multiple_of(kt * LANES, LANES), LANES)

    def slab_copy(kt):
        return pltpu.make_async_remote_copy(
            src_ref=handed.at[0, :, tile(kt)], dst_ref=slab.at[:, tile(kt)],
            send_sem=slab_send, recv_sem=slab_recv.at[kt],
            device_id=partner, device_id_type=MESH,
        )

    slab_copy(0).start()
    slab_copy(1).start()
    flag_copy.wait()

    def columns(c):
        return pl.ds(pl.multiple_of(c * col_count, col_count), col_count)

    block_rows = block.at[pl.ds(col * rows, rows)]

    def send_block(d, carry):
        c = lax.rem(col + d, n_col)
        pltpu.make_async_remote_copy(
            src_ref=slab.at[:, columns(c)], dst_ref=block_rows,
            send_sem=block_send, recv_sem=block_recv,
            device_id=(section, held_row, c), device_id_type=MESH,
        ).start()
        return carry

    per_owner = 2 * rows
    factor_rows = factor_out.reshape(k_tiles * devices * per_owner, LANES)
    all_flags = flags[...].astype(F32)
    places = lax.broadcasted_iota(jnp.int32, all_flags.shape, 1)
    own_flags = [
        jnp.sum(jnp.where(places == (held_row * n_col + col) * rows + i, all_flags, 0.0), axis=1, keepdims=True)
        for i in range(rows)
    ]

    def factor_step(kt, carry):
        wait_for(slab.at[:, tile(kt)], slab_recv.at[kt])

        @pl.when(kt + 2 < k_tiles)
        def _():
            slab_copy(kt + 2).start()

        k_flags = flags[:, tile(kt)].astype(F32)
        for i in range(rows):
            normed = norm(slab[i, tile(kt), :].astype(F32), g_in[...], 1)
            projected = lax.dot_general(
                w_cols[: 4 * hidden], normed, (((1,), (1,)), ((), ())), preferred_element_type=F32
            )
            pair_flags = k_flags * own_flags[i]
            for side in range(2):
                gates = projected[2 * side * hidden : (2 * side + 1) * hidden]
                values = projected[(2 * side + 1) * hidden : (2 * side + 2) * hidden]
                factor_f32[pl.ds(side * rows + i, hidden, stride=per_owner), :] = (
                    jax.nn.sigmoid(gates) * values * pair_flags
                )
        begin = pl.multiple_of(kt * (devices * per_owner), devices * per_owner)
        factor_rows[pl.ds(begin, devices * per_owner), :] = factor_f32[...].astype(BF16)

        def send(d, c):
            r = lax.rem(row + d, n_row)
            for parity in range(2):
                z = r // 2
                low = pair_base(z, lax.rem(core + parity, 2))
                turn = lax.rem(plane - low + half - 1 + ring, ring)
                near = lax.rem(low + turn // half, ring) * 2 + lax.rem(r, 2)
                place = (lax.rem(turn, half) * 2 + 1 - side_y) * n_col + col
                target = factors.at[
                    pl.ds(0, 2), lax.rem(z - low + ring, ring), kt, pl.ds(place * (rows // 2), rows // 2)
                ]
                for e in range(parity, n_col, 2):
                    channel_col = lax.rem(col + e, n_col)
                    source = factor_out.at[kt, r * n_col + channel_col]

                    def remote(source=source, target=target, near=near, channel_col=channel_col):
                        pltpu.make_async_remote_copy(
                            src_ref=source, dst_ref=target,
                            send_sem=factor_send, recv_sem=factor_recv.at[kt],
                            device_id=(section, near, channel_col), device_id_type=MESH,
                        ).start()

                    if e:
                        remote()
                    else:
                        pl.when(near != row)(remote)

                        @pl.when(near == row)
                        def _(source=source, target=target):
                            pltpu.make_async_copy(source, target, factor_recv.at[kt]).start()

            return c

        lax.fori_loop(0, n_row, send, 0)
        return carry

    lax.fori_loop(0, k_tiles, factor_step, 0)

    lax.fori_loop(0, n_col, send_block, 0)

    span = size // 2
    arrived = factors.reshape(3 * 2 * k_tiles * span, LANES)

    def product_step(first, which, kt):
        for channel in range(2):
            def operand(kind):
                begin = ((kind * 2 + channel) * k_tiles + kt) * span
                return arrived[pl.ds(pl.multiple_of(begin, span), span), :]

            part = lax.dot_general(
                operand(0), operand(1 + which), (((1,), (1,)), ((), ())), preferred_element_type=F32
            )
            spot = (slice(channel * span, (channel + 1) * span), slice(which * span, (which + 1) * span))
            products[spot] = part if first else products[spot] + part

    def twin_copy(kt):
        return pltpu.make_async_remote_copy(
            src_ref=factors.at[1, :, kt], dst_ref=factors.at[2, :, kt],
            send_sem=twin_send, recv_sem=twin_recv.at[kt],
            device_id=twin, device_id_type=MESH,
        )

    def take(kt):
        wait_for(factors.at[pl.ds(0, 2), :, kt], factor_recv.at[kt])
        twin_copy(kt).start()

    def take_twin(kt):
        wait_for(factors.at[2, :, kt], twin_recv.at[kt])

    def product_steps(kt, carry):
        take(kt)
        product_step(False, 0, kt)
        take_twin(kt - 1)
        product_step(False, 1, kt - 1)
        return carry

    take(0)
    product_step(True, 0, 0)
    take(1)
    product_step(False, 0, 1)
    take_twin(0)
    product_step(True, 1, 0)
    lax.fori_loop(2, k_tiles, product_steps, 0)

    kept = parts * part_rows
    product_rows = product_out.reshape(parts * devices * part_rows, LANES)
    spare = LANES - col_count

    def pack(part, begin_block, end_block):
        blocks = end_block - begin_block

        def step(d, carry):
            channel, group = lax.rem(d, 2), d // 2
            tile_rows = products[
                pl.ds(pl.multiple_of(channel * span + group * row_count, row_count), row_count),
                begin_block * col_count : end_block * col_count,
            ]
            for c in range(blocks):
                into = slice(c * part_rows, (c + 1) * part_rows)
                packed_f32[into, :col_count] = tile_rows[
                    part * part_rows : (part + 1) * part_rows, c * col_count : (c + 1) * col_count
                ]
                begin = c * col_count + part * spare
                packed_f32[into, col_count:] = tile_rows[kept:, begin : begin + spare]
            index = (channel * n_col + group) * n_col + begin_block
            begin = (part * devices + index) * part_rows
            product_rows[pl.ds(pl.multiple_of(begin, 4 * part_rows), blocks * part_rows), :] = (
                packed_f32[: blocks * part_rows, :].astype(BF16)
            )
            r = lax.rem(first_plane + group // 2, ring) * 2 + lax.rem(group, 2)
            own = own_channels[0] + channel * (own_channels[1] - own_channels[0])
            for m in range(begin_block, end_block):
                c = lax.rem(first_plane + m, n_col)
                source = product_out.at[part, index + (m - begin_block)]
                target = product_in.at[part, own]
                here = (r == row) & (c == col)

                @pl.when(jnp.logical_not(here))
                def _(source=source, target=target, c=c):
                    pltpu.make_async_remote_copy(
                        src_ref=source, dst_ref=target,
                        send_sem=product_send, recv_sem=product_recv.at[part],
                        device_id=(section, r, c), device_id_type=MESH,
                    ).start()

                @pl.when(here)
                def _(source=source, target=target):
                    pltpu.make_async_copy(source, target, product_recv.at[part]).start()

            return carry

        lax.fori_loop(0, n_row, step, 0)

    pack(0, 0, n_col // 2)
    take_twin(k_tiles - 1)
    product_step(False, 1, k_tiles - 1)
    pack(0, n_col // 2, n_col)
    for part in range(1, parts):
        pack(part, 0, n_col)

    wait_for(block, block_recv)

    batch = 4

    def gate_step(b, carry):
        some = pl.ds(b * batch, batch)
        flat = block[some].reshape(batch * col_count, channels)
        normed = norm(flat.astype(F32), g_in[...], 1)
        gating = jnp.dot(normed, w_in[0, :, 4 * hidden :], preferred_element_type=F32)
        gate[some] = jax.nn.sigmoid(gating).reshape(batch, col_count, channels)
        return carry

    lax.fori_loop(0, row_count // batch, gate_step, 0)
    product_in_rows = product_in.reshape(parts * devices * part_rows, LANES)
    for part in range(parts):
        wait_for(product_in.at[part], product_recv.at[part])
        product_f32[...] = product_in_rows[
            part * devices * part_rows : (part + 1) * devices * part_rows, :
        ].astype(F32)

        def finish(q, carry, part=part):
            normed = norm(product_f32[pl.ds(q, devices, stride=part_rows), :], g_cols[...], 0)
            update = lax.dot_general(
                normed, w_out[0], (((0,), (0,)), ((), ())), preferred_element_type=F32
            )
            i = part * part_rows + q
            out[0, i] = (block[i].astype(F32) + gate[i] * update[:col_count]).astype(BF16)
            i, j = kept + q, slice(part * spare, (part + 1) * spare)
            out[0, i, j] = (block[i, j].astype(F32) + gate[i, j] * update[col_count:]).astype(BF16)
            return carry

        lax.fori_loop(0, part_rows, finish, 0)

    wait_for(slab, slab_send)
    wait_for(factor_out.at[:, pl.ds(0, devices - 2)], factor_send)
    wait_for(factors.at[1], twin_send)
    wait_for(product_out.at[:, pl.ds(0, devices - 2)], product_send)
    wait_for(block, block_send)


def local(n_row, n_col, handed, residue_mask, input_weights, input_gain, product_gain, output_weights):
    _, rows, size, channels = handed.shape
    hidden = output_weights.shape[1]
    devices = n_row * n_col
    k_tiles = size // LANES
    row_count, col_count = size // n_row, size // n_col
    message = row_count * col_count // LANES
    parts = 3
    part_rows = message // parts
    vmem = pl.BlockSpec(memory_space=pltpu.VMEM)
    dma = pltpu.SemaphoreType.DMA
    return pl.pallas_call(
        functools.partial(kernel, n_row, n_col),
        out_shape=jax.ShapeDtypeStruct((1, row_count, col_count, channels), BF16),
        in_specs=[pl.BlockSpec(memory_space=pl.ANY)] * 6,
        out_specs=vmem,
        scratch_shapes=[
            pltpu.VMEM(input_weights.shape, BF16),
            pltpu.VMEM(input_gain.shape, F32),
            pltpu.VMEM(product_gain.shape, F32),
            pltpu.VMEM(output_weights.shape, BF16),
            pltpu.VMEM((rows, size, channels), BF16),
            pltpu.VMEM((1, size), jnp.int32),
            pltpu.VMEM(input_weights.shape[:0:-1], BF16),
            pltpu.VMEM((hidden, LANES), F32),
            pltpu.VMEM((devices * 2 * rows, LANES), F32),
            pltpu.VMEM((k_tiles, devices, 2, rows // 2, 2, LANES), BF16),
            pltpu.VMEM((3, 2, k_tiles, size // 4, 2, LANES), BF16),
            pltpu.VMEM((size, size), F32),
            pltpu.VMEM((n_col * part_rows, LANES), F32),
            pltpu.VMEM((parts, devices, part_rows // 2, 2, LANES), BF16),
            pltpu.VMEM((parts, devices, part_rows // 2, 2, LANES), BF16),
            pltpu.VMEM((devices * part_rows, LANES), F32),
            pltpu.VMEM((row_count, col_count, channels), BF16),
            pltpu.VMEM((row_count, col_count, channels), F32),
            dma((4,)), dma((2,)), dma, dma((k_tiles,)), dma, dma((k_tiles,)),
            dma, dma((k_tiles,)), dma, dma((parts,)), dma, dma,
        ],
        compiler_params=pltpu.CompilerParams(
            collective_id=0, has_side_effects=True, vmem_limit_bytes=61 * 2**20
        ),
    )(handed, residue_mask, input_weights, input_gain, product_gain, output_weights)


def solution(mesh):
    placed = (
        P("section", ("row", "col"), None, None),
        P("section", None),
        P("section", None, None),
        P("section", None),
        P("section", None),
        P("section", None, None),
    )
    return jax.shard_map(
        functools.partial(local, mesh.shape["row"], mesh.shape["col"]),
        mesh=mesh,
        in_specs=placed,
        out_specs=P("section", "row", "col", None),
        check_vma=False,
    )
```

```python
import functools

import jax
import jax.numpy as jnp
from jax import lax
from jax.experimental import pallas as pl
from jax.experimental.pallas import tpu as pltpu
from jax.sharding import PartitionSpec as P

EPS = 1e-05
LANES = 128
MESH = pl.DeviceIdType.MESH
BF16 = jnp.bfloat16
F32 = jnp.float32


def norm(values, gain, axis):
    center = jnp.mean(values, axis=axis, keepdims=True)
    deviate = values - center
    spread = jnp.mean(deviate * deviate, axis=axis, keepdims=True)
    return (deviate * lax.rsqrt(spread + EPS) * gain).astype(BF16)


def wait_for(ref, sem):
    pltpu.make_async_copy(ref, ref, sem).wait()


def kernel(
    n_row, n_col,
    handed, mask, w_in_hbm, g_in_hbm, g_prod_hbm, w_out_hbm, out,
    w_in, g_in, g_prod, w_out, slab, flags, w_cols, g_cols, factor_f32, factor_out, factors, products,
    packed_f32, product_out, product_in, product_f32, block, gate,
    load_sems, flag_sems, slab_send, slab_recv, factor_send, factor_recv, twin_send, twin_recv,
    product_send, product_recv, block_send, block_recv,
):
    rows, size, channels = slab.shape
    hidden = w_out.shape[1]
    k_tiles = size // LANES
    devices = n_row * n_col
    row_count, col_count = size // n_row, size // n_col
    parts, part_rows = product_out.shape[0], 2 * product_out.shape[2]
    section, row, col = (lax.axis_index(a) for a in ("section", "row", "col"))
    me = row * n_col + col

    ring = n_row // 2
    half = ring // 2
    plane, side_y, core = row // 2, lax.rem(row, 2), lax.rem(col, 2)

    held_row = plane * 2 + 1 - side_y
    partner = (1 - section, held_row, col)

    def pair_base(z, c):
        return lax.rem(lax.rem(z - c + ring, ring) // 2 * 2 + c, ring)

    base = pair_base(plane, core)
    upper = lax.rem(plane - base + ring, ring)
    first_plane = lax.rem(base + half * upper + ring + 1 - half, ring)
    twin = (section, lax.rem(base + 1 - upper, ring) * 2 + side_y, col)
    own_channels = [(lax.rem(base + i, ring) * 2 + side_y) * n_col + col for i in range(2)]

    loads = [
        pltpu.make_async_copy(source, target, load_sems.at[i])
        for i, (source, target) in enumerate(
            ((w_in_hbm, w_in), (g_prod_hbm, g_prod), (g_in_hbm, g_in), (w_out_hbm, w_out))
        )
    ]
    for load in loads:
        load.start()
    barrier = pltpu.get_barrier_semaphore()
    pl.semaphore_signal(barrier, inc=1, device_id=partner, device_id_type=MESH)

    def greet(d, carry):
        for e in range(n_col):
            r, c = lax.rem(row + d, n_row), lax.rem(col + e, n_col)

            @pl.when((d > 0) | (e > 0))
            def _():
                pl.semaphore_signal(barrier, inc=1, device_id=(section, r, c), device_id_type=MESH)

        return carry

    lax.fori_loop(0, n_row, greet, 0)
    for load in loads:
        load.wait()
    w_cols[...] = w_in[0].astype(F32).T.astype(BF16)
    g_cols[...] = jnp.broadcast_to(g_prod[...], (LANES, hidden)).T
    pl.semaphore_wait(barrier, devices)

    flag_copy = pltpu.make_async_remote_copy(
        src_ref=mask, dst_ref=flags, send_sem=flag_sems.at[0], recv_sem=flag_sems.at[1],
        device_id=partner, device_id_type=MESH,
    )
    flag_copy.start()

    def tile(kt):
        return pl.ds(pl.multiple_of(kt * LANES, LANES), LANES)

    def slab_copy(kt):
        return pltpu.make_async_remote_copy(
            src_ref=handed.at[0, :, tile(kt)], dst_ref=slab.at[:, tile(kt)],
            send_sem=slab_send, recv_sem=slab_recv.at[kt],
            device_id=partner, device_id_type=MESH,
        )

    slab_copy(0).start()
    slab_copy(1).start()
    flag_copy.wait()

    def columns(c):
        return pl.ds(pl.multiple_of(c * col_count, col_count), col_count)

    block_rows = block.at[pl.ds(col * rows, rows)]

    def send_block(d, carry):
        c = lax.rem(col + d, n_col)
        pltpu.make_async_remote_copy(
            src_ref=slab.at[:, columns(c)], dst_ref=block_rows,
            send_sem=block_send, recv_sem=block_recv,
            device_id=(section, held_row, c), device_id_type=MESH,
        ).start()
        return carry

    per_owner = 2 * rows
    factor_rows = factor_out.reshape(k_tiles * devices * per_owner, LANES)
    all_flags = flags[...].astype(F32)
    places = lax.broadcasted_iota(jnp.int32, all_flags.shape, 1)
    own_flags = [
        jnp.sum(jnp.where(places == (held_row * n_col + col) * rows + i, all_flags, 0.0), axis=1, keepdims=True)
        for i in range(rows)
    ]

    def factor_step(kt, carry):
        wait_for(slab.at[:, tile(kt)], slab_recv.at[kt])

        @pl.when(kt + 2 < k_tiles)
        def _():
            slab_copy(kt + 2).start()

        k_flags = flags[:, tile(kt)].astype(F32)
        for i in range(rows):
            normed = norm(slab[i, tile(kt), :].astype(F32), g_in[...], 1)
            projected = lax.dot_general(
                w_cols[: 4 * hidden], normed, (((1,), (1,)), ((), ())), preferred_element_type=F32
            )
            pair_flags = k_flags * own_flags[i]
            for side in range(2):
                gates = projected[2 * side * hidden : (2 * side + 1) * hidden]
                values = projected[(2 * side + 1) * hidden : (2 * side + 2) * hidden]
                factor_f32[pl.ds(side * rows + i, hidden, stride=per_owner), :] = (
                    jax.nn.sigmoid(gates) * values * pair_flags
                )
        begin = pl.multiple_of(kt * (devices * per_owner), devices * per_owner)
        factor_rows[pl.ds(begin, devices * per_owner), :] = factor_f32[...].astype(BF16)

        def send(d, c):
            r = lax.rem(row + d, n_row)
            for parity in range(2):
                z = r // 2
                low = pair_base(z, lax.rem(core + parity, 2))
                turn = lax.rem(plane - low + half - 1 + ring, ring)
                near = lax.rem(low + turn // half, ring) * 2 + lax.rem(r, 2)
                place = (lax.rem(turn, half) * 2 + 1 - side_y) * n_col + col
                target = factors.at[
                    pl.ds(0, 2), lax.rem(z - low + ring, ring), kt, pl.ds(place * (rows // 2), rows // 2)
                ]
                for e in range(parity, n_col, 2):
                    channel_col = lax.rem(col + e, n_col)
                    source = factor_out.at[kt, r * n_col + channel_col]

                    def remote(source=source, target=target, near=near, channel_col=channel_col):
                        pltpu.make_async_remote_copy(
                            src_ref=source, dst_ref=target,
                            send_sem=factor_send, recv_sem=factor_recv.at[kt],
                            device_id=(section, near, channel_col), device_id_type=MESH,
                        ).start()

                    if e:
                        remote()
                    else:
                        pl.when(near != row)(remote)

                        @pl.when(near == row)
                        def _(source=source, target=target):
                            pltpu.make_async_copy(source, target, factor_recv.at[kt]).start()

            return c

        lax.fori_loop(0, n_row, send, 0)
        return carry

    lax.fori_loop(0, k_tiles, factor_step, 0)

    lax.fori_loop(0, n_col, send_block, 0)

    span = size // 2
    arrived = factors.reshape(3 * 2 * k_tiles * span, LANES)

    def product_step(first, which, kt):
        for channel in range(2):
            def operand(kind):
                begin = ((kind * 2 + channel) * k_tiles + kt) * span
                return arrived[pl.ds(pl.multiple_of(begin, span), span), :]

            part = lax.dot_general(
                operand(0), operand(1 + which), (((1,), (1,)), ((), ())), preferred_element_type=F32
            )
            spot = (slice(channel * span, (channel + 1) * span), slice(which * span, (which + 1) * span))
            products[spot] = part if first else products[spot] + part

    def twin_copy(kt):
        return pltpu.make_async_remote_copy(
            src_ref=factors.at[1, :, kt], dst_ref=factors.at[2, :, kt],
            send_sem=twin_send, recv_sem=twin_recv.at[kt],
            device_id=twin, device_id_type=MESH,
        )

    def take(kt):
        wait_for(factors.at[pl.ds(0, 2), :, kt], factor_recv.at[kt])
        twin_copy(kt).start()

    def take_twin(kt):
        wait_for(factors.at[2, :, kt], twin_recv.at[kt])

    def product_steps(kt, carry):
        take(kt)
        product_step(False, 0, kt)
        take_twin(kt - 1)
        product_step(False, 1, kt - 1)
        return carry

    take(0)
    product_step(True, 0, 0)
    take(1)
    product_step(False, 0, 1)
    take_twin(0)
    product_step(True, 1, 0)
    lax.fori_loop(2, k_tiles, product_steps, 0)

    kept = parts * part_rows
    product_rows = product_out.reshape(parts * devices * part_rows, LANES)
    spare = LANES - col_count

    def pack(part, begin_block, end_block):
        blocks = end_block - begin_block

        def step(d, carry):
            channel, group = lax.rem(d, 2), d // 2
            tile_rows = products[
                pl.ds(pl.multiple_of(channel * span + group * row_count, row_count), row_count),
                begin_block * col_count : end_block * col_count,
            ]
            for c in range(blocks):
                into = slice(c * part_rows, (c + 1) * part_rows)
                packed_f32[into, :col_count] = tile_rows[
                    part * part_rows : (part + 1) * part_rows, c * col_count : (c + 1) * col_count
                ]
                begin = c * col_count + part * spare
                packed_f32[into, col_count:] = tile_rows[kept:, begin : begin + spare]
            index = (channel * n_col + group) * n_col + begin_block
            begin = (part * devices + index) * part_rows
            product_rows[pl.ds(pl.multiple_of(begin, 4 * part_rows), blocks * part_rows), :] = (
                packed_f32[: blocks * part_rows, :].astype(BF16)
            )
            r = lax.rem(first_plane + group // 2, ring) * 2 + lax.rem(group, 2)
            own = own_channels[0] + channel * (own_channels[1] - own_channels[0])
            for m in range(begin_block, end_block):
                c = lax.rem(first_plane + m, n_col)
                source = product_out.at[part, index + (m - begin_block)]
                target = product_in.at[part, own]
                here = (r == row) & (c == col)

                @pl.when(jnp.logical_not(here))
                def _(source=source, target=target, c=c):
                    pltpu.make_async_remote_copy(
                        src_ref=source, dst_ref=target,
                        send_sem=product_send, recv_sem=product_recv.at[part],
                        device_id=(section, r, c), device_id_type=MESH,
                    ).start()

                @pl.when(here)
                def _(source=source, target=target):
                    pltpu.make_async_copy(source, target, product_recv.at[part]).start()

            return carry

        lax.fori_loop(0, n_row, step, 0)

    pack(0, 0, n_col // 2)
    take_twin(k_tiles - 1)
    product_step(False, 1, k_tiles - 1)
    pack(0, n_col // 2, n_col)
    for part in range(1, parts):
        pack(part, 0, n_col)

    wait_for(block, block_recv)

    batch = 4

    def gate_step(b, carry):
        some = pl.ds(b * batch, batch)
        flat = block[some].reshape(batch * col_count, channels)
        normed = norm(flat.astype(F32), g_in[...], 1)
        gating = jnp.dot(normed, w_in[0, :, 4 * hidden :], preferred_element_type=F32)
        gate[some] = jax.nn.sigmoid(gating).reshape(batch, col_count, channels)
        return carry

    lax.fori_loop(0, row_count // batch, gate_step, 0)
    product_in_rows = product_in.reshape(parts * devices * part_rows, LANES)
    for part in range(parts):
        wait_for(product_in.at[part], product_recv.at[part])
        product_f32[...] = product_in_rows[
            part * devices * part_rows : (part + 1) * devices * part_rows, :
        ].astype(F32)

        def finish(q, carry, part=part):
            normed = norm(product_f32[pl.ds(q, devices, stride=part_rows), :], g_cols[...], 0)
            update = lax.dot_general(
                normed, w_out[0], (((0,), (0,)), ((), ())), preferred_element_type=F32
            )
            i = part * part_rows + q
            out[0, i] = (block[i].astype(F32) + gate[i] * update[:col_count]).astype(BF16)
            i, j = kept + q, slice(part * spare, (part + 1) * spare)
            out[0, i, j] = (block[i, j].astype(F32) + gate[i, j] * update[col_count:]).astype(BF16)
            return carry

        lax.fori_loop(0, part_rows, finish, 0, unroll=6)

    wait_for(slab, slab_send)
    wait_for(factor_out.at[:, pl.ds(0, devices - 2)], factor_send)
    wait_for(factors.at[1], twin_send)
    wait_for(product_out.at[:, pl.ds(0, devices - 2)], product_send)
    wait_for(block, block_send)


def local(n_row, n_col, handed, residue_mask, input_weights, input_gain, product_gain, output_weights):
    _, rows, size, channels = handed.shape
    hidden = output_weights.shape[1]
    devices = n_row * n_col
    k_tiles = size // LANES
    row_count, col_count = size // n_row, size // n_col
    message = row_count * col_count // LANES
    parts = 3
    part_rows = message // parts
    vmem = pl.BlockSpec(memory_space=pltpu.VMEM)
    dma = pltpu.SemaphoreType.DMA
    return pl.pallas_call(
        functools.partial(kernel, n_row, n_col),
        out_shape=jax.ShapeDtypeStruct((1, row_count, col_count, channels), BF16),
        in_specs=[pl.BlockSpec(memory_space=pl.ANY)] * 6,
        out_specs=vmem,
        scratch_shapes=[
            pltpu.VMEM(input_weights.shape, BF16),
            pltpu.VMEM(input_gain.shape, F32),
            pltpu.VMEM(product_gain.shape, F32),
            pltpu.VMEM(output_weights.shape, BF16),
            pltpu.VMEM((rows, size, channels), BF16),
            pltpu.VMEM((1, size), jnp.int32),
            pltpu.VMEM(input_weights.shape[:0:-1], BF16),
            pltpu.VMEM((hidden, LANES), F32),
            pltpu.VMEM((devices * 2 * rows, LANES), F32),
            pltpu.VMEM((k_tiles, devices, 2, rows // 2, 2, LANES), BF16),
            pltpu.VMEM((3, 2, k_tiles, size // 4, 2, LANES), BF16),
            pltpu.VMEM((size, size), F32),
            pltpu.VMEM((n_col * part_rows, LANES), F32),
            pltpu.VMEM((parts, devices, part_rows // 2, 2, LANES), BF16),
            pltpu.VMEM((parts, devices, part_rows // 2, 2, LANES), BF16),
            pltpu.VMEM((devices * part_rows, LANES), F32),
            pltpu.VMEM((row_count, col_count, channels), BF16),
            pltpu.VMEM((row_count, col_count, channels), F32),
            dma((4,)), dma((2,)), dma, dma((k_tiles,)), dma, dma((k_tiles,)),
            dma, dma((k_tiles,)), dma, dma((parts,)), dma, dma,
        ],
        compiler_params=pltpu.CompilerParams(
            collective_id=0, has_side_effects=True, vmem_limit_bytes=61 * 2**20
        ),
    )(handed, residue_mask, input_weights, input_gain, product_gain, output_weights)


def solution(mesh):
    placed = (
        P("section", ("row", "col"), None, None),
        P("section", None),
        P("section", None, None),
        P("section", None),
        P("section", None),
        P("section", None, None),
    )
    return jax.shard_map(
        functools.partial(local, mesh.shape["row"], mesh.shape["col"]),
        mesh=mesh,
        in_specs=placed,
        out_specs=P("section", "row", "col", None),
        check_vma=False,
    )
```
